32 devices in a mesh: parts: 2 (over y), tm: 4 (over z), chan: 2 (over x), sub: 2 (over core).
Axes of the slice: x: 2, y: 2, z: 4, core: 2. Of those that a mesh axis runs over, the one named last changes fastest.
Arguments:
- start_state: float32 [16, 2048], P(('parts', 'chan')), parts along dimension 0, may hold values from -6 to 6
- guess: bfloat16 [64, 8, 2048], P(('parts', 'tm', 'sub'), 'chan'), parts along dimension 0, may hold values from -6 to 6
- w_in: bfloat16 [576, 320], replicated, may hold values from -0.25 to 0.25
- w_mid: bfloat16 [2880, 320], replicated, may hold values from -0.109375 to 0.109375
- w_out: bfloat16 [2880, 64], replicated, may hold values from -0.875 to 0.875
- time_embed: bfloat16 [1000, 320], replicated, may hold values from -4 to 4
- levels: float32 [1000], replicated, may hold values from 0 to 70, as said below
- plan: int32 [130], P('parts'), parts along dimension 0, may hold values from 0 to 999, as said below
- offset: int32 [2], P('parts'), parts along dimension 0, may hold values from 0 to 32
Outputs:
- trajectory: float32 [64, 8, 2048], P(('parts', 'tm', 'sub'), 'chan'), parts along dimension 0
The draws below stay inside these ranges and needn't reach their ends.
There are 2 independent parts, one for each index of `parts`. The reference program is written for one: setup_inputs(seed, part) draws one part's arguments, and reference() takes and returns one part's arrays. A program takes and returns all parts, laid end to end along the dimension named above; an argument that names none is the same for every part. Nothing has to cross between parts.
Inputs may be any that keep to these rules, and one draw needn't show every extreme that they name: `levels`: rises strictly with the timestep, by at most 0.07 from one timestep to the next. Strictly falling along the plan; the first entry is 999 and the last is 0.
All inputs are finite; a program needn't handle non-finite values.
Results may differ from the reference program's by a relative error of at most 0.003.
Values may be sent and summed in bfloat16 or wider, within the bound.
A program may use at most 64 MiB of HBM per device.

```python
import jax
import jax.numpy as jnp
from jax import lax

C = 64
HID = 320
WT = 32
NT = 1000
ITERS = 2
H = 8
W = 32
SCHED = 64


def draw_levels(key, part):
    rises = jax.random.uniform(key, (NT,), jnp.float32, 0.02, 0.07)
    return jnp.cumsum(rises)


def draw_plan(key, part):
    inner = jax.random.permutation(key, NT - 2)[:SCHED - 1].astype(jnp.int32) + 1
    ends = jnp.array([0, NT - 1], dtype=jnp.int32)
    picked = jnp.concatenate([inner, ends])
    return (-jnp.sort(-picked)).astype(jnp.int32)


def level_of(key, shape, cuts, smallest, high):
    def one(position, parts):
        steps = jax.random.uniform(jax.random.fold_in(jax.random.fold_in(key, 6), position), (parts,), jnp.float32, smallest / len(cuts), high / len(cuts))
        return jnp.repeat(jnp.exp(steps), shape[position] // parts).reshape((-1,) + (1,) * (len(shape) - position - 1))

    factor_of = one(*cuts[0])
    for cut in cuts[1:]:
        factor_of = factor_of * one(*cut)
    return factor_of


def normal_values(stream_key, extent, deviation, limit, split=(), kind=jnp.bfloat16):
    values = deviation * jax.random.normal(stream_key, extent, jnp.float32)
    if split:
        values = values * level_of(stream_key, extent, split, -0.22, 0.18)
    return jnp.clip(values, -limit, limit).astype(kind)


def setup_inputs(seed: int = 0, part: int = 0) -> dict:
    key_of = jax.random.split(jax.random.key(seed), 10)
    part_splits = jax.random.split(jax.random.fold_in(key_of[9], part), 10)
    return {
        "start_state": normal_values(part_splits[0], (H, WT * C), 1.0, 6.0, ((0, 2),), jnp.float32),
        "guess": normal_values(part_splits[1], (W, H, WT * C), 1.0, 6.0, ((0, 8), (1, 2))),
        "w_in": normal_values(key_of[2], (9 * C, HID), (9 * C) ** -0.5, 0.25),
        "w_mid": normal_values(key_of[3], (9 * HID, HID), (9 * HID) ** -0.5, 0.109375),
        "w_out": normal_values(key_of[4], (9 * HID, C), (9 * HID // 64) ** -0.5, 0.875),
        "time_embed": normal_values(key_of[5], (NT, HID), 1.0, 4.0),
        "levels": draw_levels(jax.random.fold_in(key_of[9], 71), part),
        "plan": draw_plan(jax.random.fold_in(jax.random.fold_in(key_of[9], part), 71), part),
        "offset": jax.random.randint(part_splits[8], (1,), 0, W + 1).astype(jnp.int32),
    }


def conv_same(layer_in, weight):
    channels = layer_in.shape[-1]
    kernel = weight.astype(jnp.float32).reshape(3, 3, channels, weight.shape[1])
    return lax.conv_general_dilated(layer_in, kernel, (1, 1), "SAME", dimension_numbers=("NHWC", "HWIO", "NHWC"), precision=lax.Precision.HIGHEST)


def drift_block(layer_in, embed, w_in, w_mid, w_out):
    block_steps, tile_rows, merged = layer_in.shape
    channels = w_out.shape[1]
    tiles = layer_in.astype(jnp.float32).reshape(block_steps, tile_rows, merged // channels, channels)
    first_hidden = jax.nn.silu(conv_same(tiles, w_in) + embed[:, None, None, :]).astype(jnp.bfloat16)
    first_hidden = lax.optimization_barrier(first_hidden).astype(jnp.float32)
    second_hidden = jax.nn.silu(conv_same(first_hidden, w_mid)).astype(jnp.bfloat16)
    second_hidden = lax.optimization_barrier(second_hidden).astype(jnp.float32)
    drift_out = conv_same(second_hidden, w_out)
    return drift_out.reshape(block_steps, tile_rows, merged)


def reference(start_state, guess, w_in, w_mid, w_out, time_embed, levels, plan, offset):
    window = guess.shape[0]
    window_ids = lax.dynamic_slice_in_dim(plan, offset[0].astype(jnp.int32), window + 1)
    noise = levels[window_ids]
    step_size = noise[1:] - noise[:-1]
    embed = time_embed[window_ids[:-1]].astype(jnp.float32)
    factor = jnp.where(jnp.arange(window) == 0, 1.0, 1.5).astype(jnp.float32)
    layer_in = guess
    states_after = None
    for sweep in range(ITERS):
        blocks = layer_in.reshape(window // 8, 8, guess.shape[1], guess.shape[2])
        embed_blocks = embed.reshape(window // 8, 8, embed.shape[1])
        drift_all = lax.map(lambda pair: drift_block(pair[0], pair[1], w_in, w_mid, w_out), (blocks, embed_blocks))
        drift_all = drift_all.reshape(guess.shape)
        earlier = jnp.concatenate([jnp.zeros_like(drift_all[:1]), drift_all[:-1]], axis=0)
        increment = step_size[:, None, None] * (factor[:, None, None] * drift_all - 0.5 * earlier)
        running = jnp.cumsum(increment, axis=0)
        states_after = start_state[None] + running
        states_before = states_after - increment
        layer_in = states_before.astype(jnp.bfloat16)
    return states_after
```

```python
import functools

import jax
import jax.numpy as jnp
from jax import lax
from jax.experimental import pallas as pl
from jax.experimental.pallas import tpu as pltpu
from jax.sharding import PartitionSpec as P

ITERS = 2
MESH = pl.DeviceIdType.MESH
F32 = jnp.float32
BF16 = jnp.bfloat16


def silu(v):
    half = 0.5 * v
    return half + half * jnp.tanh(half)


def fold(array):
    half = array.shape[0] // 2
    return jnp.concatenate([array[:half], array[half:]], axis=1)


def unfold(array):
    half = array.shape[1] // 2
    return jnp.concatenate([array[:, :half], array[:, half:]], axis=0)


def body(
    cfg,
    start_ref, guess_ref, levels_ref, plan_ref, offset_ref, w_in_hbm, w_mid_hbm, w_out_hbm, te_hbm,
    out_ref,
    w_in, w_mid, w_out, te, w_sum, x1, x2, x3, u_scr, st_scr, o_scr, p_scr,
    halo_send, halo_recv, t_send, t_recv, s_send, s_recv, d_send, d_recv,
    w_sem, hs_sem, hr_sem, ts_sem, tr_sem, ss_sem, sr_sem, ds_sem, dr_sem,
):
    steps, rows, cols, ch, hid, n_chan, n_tm, n_levels, n_plan, two = cfg
    block = steps * cols
    z = lax.axis_index("tm")
    sub = lax.axis_index("sub")
    chan = lax.axis_index("chan")
    first = (z * 2 + sub) * steps
    has_low = chan > 0
    has_high = chan < n_chan - 1

    weights = [
        pltpu.make_async_copy(src, dst, w_sem.at[i])
        for i, (src, dst) in enumerate(
            [(w_in_hbm, w_in), (te_hbm, te), (w_mid_hbm, w_mid), (w_out_hbm, w_out)]
        )
    ]
    for copy in weights:
        copy.start()

    barrier = pltpu.get_barrier_semaphore()
    next_z = (sub == 1) & (z < n_tm - 1)
    prev_z = (sub == 0) & (z > 0)

    def hello(dev):
        pl.semaphore_signal(barrier, inc=1, device_id=dev, device_id_type=MESH)

    hello({"sub": 1 - sub})
    for k in range(n_tm):
        @pl.when(k != z)
        def _():
            hello({"tm": k})
    @pl.when(next_z)
    def _():
        hello({"tm": z + 1, "sub": 0})
    @pl.when(prev_z)
    def _():
        hello({"tm": z - 1, "sub": 1})
    @pl.when(has_low)
    def _():
        hello({"chan": chan - 1})
    @pl.when(has_high)
    def _():
        hello({"chan": chan + 1})

    for n in range(steps):
        tile = guess_ref[n].astype(F32)
        for c in range(cols):
            u_scr[pl.ds(n * cols + c, rows, stride=block), :] = tile[:, c * ch:(c + 1) * ch]
    for c in range(cols):
        st_scr[pl.ds(c, rows, stride=cols), :] = start_ref[:, c * ch:(c + 1) * ch]

    own = (1 + 2 * chan) if two else 3
    n_in = rows + 4 if two else rows + 6
    n1, n2 = n_in - 2, (n_in - 3 if two else n_in - 4)
    o1 = (1 - chan) if two else 0
    if two:
        x1[pl.ds(pl.multiple_of(chan * (n_in - 1) * block, block), block), :] = jnp.zeros((block, 3 * ch), BF16)
        x2[pl.ds(pl.multiple_of(chan * n1 * block, block), block), :] = jnp.zeros((block, 3 * hid), BF16)
        x3[pl.ds(pl.multiple_of(chan * n2 * block, block), block), :] = jnp.zeros((block, 3 * hid), BF16)
    else:
        x1[...] = jnp.zeros(x1.shape, BF16)

    pl.semaphore_wait(
        barrier,
        n_tm + next_z.astype(jnp.int32) + prev_z.astype(jnp.int32)
        + has_low.astype(jnp.int32) + has_high.astype(jnp.int32),
    )

    def halo_copy(sweep, side):
        return pltpu.make_async_remote_copy(
            src_ref=halo_send.at[sweep, side], dst_ref=halo_recv.at[sweep, side],
            send_sem=hs_sem.at[sweep, side], recv_sem=hr_sem.at[sweep, side],
            device_id={"chan": chan - 1 + 2 * side}, device_id_type=MESH,
        )

    def t_copy(sweep, target):
        return pltpu.make_async_remote_copy(
            src_ref=t_send.at[sweep], dst_ref=t_recv.at[sweep, z],
            send_sem=ts_sem.at[sweep, target], recv_sem=tr_sem.at[sweep, z],
            device_id={"tm": target}, device_id_type=MESH,
        )

    def t_arrived(sweep, source):
        return pltpu.make_async_remote_copy(
            src_ref=t_send.at[sweep], dst_ref=t_recv.at[sweep, source],
            send_sem=ts_sem.at[sweep, source], recv_sem=tr_sem.at[sweep, source],
            device_id={"tm": source}, device_id_type=MESH,
        )

    def s_copy(sweep):
        return pltpu.make_async_remote_copy(
            src_ref=s_send.at[sweep], dst_ref=s_recv.at[sweep],
            send_sem=ss_sem.at[sweep], recv_sem=sr_sem.at[sweep],
            device_id={"sub": 1 - sub}, device_id_type=MESH,
        )

    def d_copy(dev):
        return pltpu.make_async_remote_copy(
            src_ref=d_send, dst_ref=d_recv, send_sem=ds_sem, recv_sem=dr_sem,
            device_id=dev, device_id_type=MESH,
        )

    edge = 3 * block

    def send_halo(sweep):
        halo_send[sweep, 0] = fold(u_scr[0:edge, :]).astype(BF16)
        halo_send[sweep, 1] = fold(u_scr[rows * block - edge:rows * block, :]).astype(BF16)
        for side, there in ((0, has_low), (1, has_high)):
            @pl.when(there)
            def _():
                halo_copy(sweep, side).start()

    send_halo(0)

    base = offset_ref[0] + first
    ids = [plan_ref[jnp.minimum(base + n, n_plan - 1)] for n in range(steps + 2)]
    noise = [levels_ref[i] for i in ids]
    size = [noise[n + 1] - noise[n] for n in range(steps + 1)]
    front = [size[n] * jnp.where(first + n == 0, 1.0, 1.5) for n in range(steps)]
    onward = [front[n] - 0.5 * size[n + 1] for n in range(steps)]

    col_of = lax.broadcasted_iota(jnp.int32, (block, 1), 0) % cols

    def spread(value):
        left = jnp.where(col_of == 0, 0.0, pltpu.roll(value, 1, 0))
        right = jnp.where(col_of == cols - 1, 0.0, pltpu.roll(value, block - 1, 0))
        return jnp.concatenate([left, value, right], axis=1).astype(BF16)

    def at(row):
        if isinstance(row, int):
            return pl.ds(row * block, block)
        return pl.ds(pl.multiple_of(row * block, block), block)

    def chosen(n_rows, first_row, r):
        position = chan * rows + first_row + r
        return ((position >= 0) & (position < n_chan * rows)).astype(F32)

    def own_rows():
        for r in range(rows):
            x1[at(own + r), :] = spread(u_scr[r * block:(r + 1) * block, :])

    own_rows()
    weights[0].wait()
    weights[1].wait()
    hot = jnp.zeros((8, n_levels), F32)
    row_of = lax.broadcasted_iota(jnp.int32, (8, n_levels), 0)
    id_of = lax.broadcasted_iota(jnp.int32, (8, n_levels), 1)
    for n in range(steps):
        hot = jnp.where((row_of == n) & (id_of == ids[n]), 1.0, hot)
    embed8 = jnp.dot(hot.astype(BF16), te[...], preferred_element_type=F32)
    embed = jnp.concatenate(
        [jnp.broadcast_to(embed8[n:n + 1], (cols, hid)) for n in range(steps)], axis=0
    )

    for sweep in range(ITERS):
        for side, there in ((1, has_low), (0, has_high)):
            @pl.when(there)
            def _():
                halo_copy(sweep, side).wait_recv()
                got = unfold(halo_recv[sweep, side].astype(F32))
                for r in range(3):
                    x1[at(r if side == 1 else own + rows + r), :] = spread(got[r * block:(r + 1) * block])
        act = jnp.dot(x1[0:n1 * block, :], w_in[0:3 * ch, :], preferred_element_type=F32)
        for kr in (1, 2):
            act += jnp.dot(
                x1[kr * block:(kr + n1) * block, :], w_in[kr * 3 * ch:(kr + 1) * 3 * ch, :],
                preferred_element_type=F32,
            )
        for r in range(n1):
            hidden = silu(act[r * block:(r + 1) * block] + embed)
            if not two:
                hidden = hidden * chosen(n1, -2, r)
            x2[at(o1 + r), :] = spread(hidden)
        if sweep == 0:
            weights[2].wait()
        act = jnp.dot(x2[0:n2 * block, :], w_mid[0:3 * hid, :], preferred_element_type=F32)
        for kr in (1, 2):
            act += jnp.dot(
                x2[kr * block:(kr + n2) * block, :], w_mid[kr * 3 * hid:(kr + 1) * 3 * hid, :],
                preferred_element_type=F32,
            )
        for r in range(n2):
            hidden = silu(act[r * block:(r + 1) * block])
            if not two:
                hidden = hidden * chosen(n2, -1, r)
            x3[at(o1 + r), :] = spread(hidden)
        if sweep == 0:
            weights[3].wait()
            for kr in range(3):
                w_sum[:, kr * ch:(kr + 1) * ch] = w_out[kr * 3 * hid:(kr + 1) * 3 * hid, :]
        taps = jnp.dot(x3[...], w_sum[...], preferred_element_type=F32)
        size_out = rows * block
        drift = (
            taps[0:size_out, 0:ch]
            + taps[block:block + size_out, ch:2 * ch]
            + taps[2 * block:2 * block + size_out, 2 * ch:3 * ch]
        ).reshape(rows, steps, cols, ch)

        total = jnp.zeros((rows, cols, ch), F32)
        after = []
        for n in range(steps):
            after.append(total + front[n] * drift[:, n])
            total = total + onward[n] * drift[:, n]
        last = sweep == ITERS - 1
        total = fold(total.reshape(rows * cols, ch))
        t_send[sweep] = total
        for k in range(1, n_tm):
            @pl.when(k > z)
            def _():
                t_copy(sweep, k).start()
        if not last:
            d_send[...] = fold(drift[:, steps - 1].reshape(rows * cols, ch))
            @pl.when(sub == 0)
            def _():
                d_copy({"sub": 1}).start()
            @pl.when(next_z)
            def _():
                d_copy({"tm": z + 1, "sub": 0}).start()
        p_scr[...] = jnp.zeros(p_scr.shape, F32)
        for k in range(n_tm - 1):
            @pl.when(k < z)
            def _():
                t_arrived(sweep, k).wait_recv()
                p_scr[...] += t_recv[sweep, k]
        s_send[sweep] = p_scr[...] + jnp.where(sub == 0, total, 0.0)
        s_copy(sweep).start()
        s_copy(sweep).wait_recv()
        origin = st_scr[...].reshape(rows, cols, ch) + unfold(
            p_scr[...] + s_recv[sweep]
        ).reshape(rows, cols, ch)
        if last:
            for n in range(steps):
                o_scr[n * rows * cols:(n + 1) * rows * cols, :] = (origin + after[n]).reshape(rows * cols, ch)
            for c in range(0, cols, 2):
                out_ref[:, c * ch:(c + 2) * ch] = jnp.concatenate(
                    [o_scr[pl.ds(c + i, steps * rows, stride=cols), :] for i in range(2)], axis=1
                )
        else:
            p_scr[...] = jnp.zeros(p_scr.shape, F32)
            @pl.when((sub == 1) | prev_z)
            def _():
                d_copy({"sub": 1 - sub}).wait_recv()
                p_scr[...] = d_recv[...]
            behind = unfold(p_scr[...]).reshape(rows, cols, ch)
            before = [origin + (0.5 * size[0]) * behind] + [origin + a for a in after[:-1]]
            for r in range(rows):
                for n in range(steps):
                    start = r * block + n * cols
                    u_scr[start:start + cols, :] = before[n][r].astype(BF16).astype(F32)
            send_halo(sweep + 1)
            own_rows()

    for sweep in range(ITERS):
        for side, there in ((0, has_low), (1, has_high)):
            @pl.when(there)
            def _():
                halo_copy(sweep, side).wait_send()
        for k in range(1, n_tm):
            @pl.when(k > z)
            def _():
                t_copy(sweep, k).wait_send()
        s_copy(sweep).wait_send()
    @pl.when((sub == 0) | next_z)
    def _():
        d_copy({"sub": 1 - sub}).wait_send()


def shards(n_chan, n_tm, start_state, guess, w_in, w_mid, w_out, time_embed, levels, plan, offset):
    steps, rows, merged = guess.shape
    ch = w_out.shape[1]
    hid = w_in.shape[1]
    cols = merged // ch
    block = steps * cols
    two = n_chan == 2
    cfg = (steps, rows, cols, ch, hid, n_chan, n_tm, levels.shape[0], plan.shape[0], two)
    n_in = rows + 4 if two else rows + 6
    n_x2 = n_in - 1 if two else n_in - 2
    n_x3 = n_in - 2 if two else n_in - 4
    vmem = pl.BlockSpec(memory_space=pltpu.VMEM)
    smem = pl.BlockSpec(memory_space=pltpu.SMEM)
    anyw = pl.BlockSpec(memory_space=pl.ANY)
    dma = pltpu.SemaphoreType.DMA
    half = rows * cols // 2
    out = pl.pallas_call(
        functools.partial(body, cfg),
        out_shape=jax.ShapeDtypeStruct((steps * rows, merged), F32),
        in_specs=[vmem, vmem, smem, smem, smem, anyw, anyw, anyw, anyw],
        out_specs=vmem,
        scratch_shapes=[
            pltpu.VMEM(w_in.shape, BF16),
            pltpu.VMEM(w_mid.shape, BF16),
            pltpu.VMEM(w_out.shape, BF16),
            pltpu.VMEM(time_embed.shape, BF16),
            pltpu.VMEM((3 * hid, 3 * ch), BF16),
            pltpu.VMEM((n_in * block, 3 * ch), BF16),
            pltpu.VMEM((n_x2 * block, 3 * hid), BF16),
            pltpu.VMEM((n_x3 * block, 3 * hid), BF16),
            pltpu.VMEM((rows * block, ch), F32),
            pltpu.VMEM((rows * cols, ch), F32),
            pltpu.VMEM((rows * block, ch), F32),
            pltpu.VMEM((half, 2 * ch), F32),
            pltpu.VMEM((ITERS, 2, 3 * block // 2, 2 * ch), BF16),
            pltpu.VMEM((ITERS, 2, 3 * block // 2, 2 * ch), BF16),
            pltpu.VMEM((ITERS, half, 2 * ch), F32),
            pltpu.VMEM((ITERS, n_tm, half, 2 * ch), F32),
            pltpu.VMEM((ITERS, half, 2 * ch), F32),
            pltpu.VMEM((ITERS, half, 2 * ch), F32),
            pltpu.VMEM((half, 2 * ch), F32),
            pltpu.VMEM((half, 2 * ch), F32),
            dma((4,)),
            dma((ITERS, 2)),
            dma((ITERS, 2)),
            dma((ITERS, n_tm)),
            dma((ITERS, n_tm)),
            dma((ITERS,)),
            dma((ITERS,)),
            dma,
            dma,
        ],
        compiler_params=pltpu.CompilerParams(
            collective_id=0, has_side_effects=True, vmem_limit_bytes=40 * 1024 * 1024
        ),
    )(start_state, guess, levels, plan, offset, w_in, w_mid, w_out, time_embed)
    return out.reshape(guess.shape)


def solution(mesh):
    return jax.shard_map(
        functools.partial(shards, mesh.shape["chan"], mesh.shape["tm"]),
        mesh=mesh,
        in_specs=(
            P(("parts", "chan"), None),
            P(("parts", "tm", "sub"), "chan", None),
            P(),
            P(),
            P(),
            P(),
            P(),
            P("parts"),
            P("parts"),
        ),
        out_specs=P(("parts", "tm", "sub"), "chan", None),
        check_vma=False,
    )
```

```python
import functools

import jax
import jax.numpy as jnp
from jax import lax
from jax.experimental import pallas as pl
from jax.experimental.pallas import tpu as pltpu
from jax.sharding import PartitionSpec as P

ITERS = 2
MESH = pl.DeviceIdType.MESH
F32 = jnp.float32
BF16 = jnp.bfloat16


def silu(v):
    half = 0.5 * v
    return half + half * jnp.tanh(half)


def dot(left, right):
    return lax.dot_general(left, right, (((1,), (1,)), ((), ())), preferred_element_type=F32)


def fold(array):
    half = array.shape[0] // 2
    return jnp.concatenate([array[:half], array[half:]], axis=1)


def unfold(array):
    half = array.shape[1] // 2
    return jnp.concatenate([array[:, :half], array[:, half:]], axis=0)


def body(
    cfg,
    start_hbm, guess_hbm, levels_hbm, plan_hbm, offset_hbm, w_in_hbm, w_mid_hbm, w_out_hbm, te_hbm,
    out_ref,
    start_ref, guess_ref, levels_ref, plan_ref, offset_ref,
    w_in_raw, w_mid_raw, w_out_raw, te, w_in, w_mid, w_sum, x1, x2, x3, u_scr, st_scr, o_scr, p_scr,
    halo_send, halo_recv, t_send, t_recv, s_send, s_recv, d_send, d_recv,
    w_sem, hs_sem, hr_sem, ts_sem, tr_sem, ss_sem, sr_sem, ds_sem, dr_sem,
):
    steps, rows, cols, ch, hid, n_chan, n_tm, n_levels, n_plan, two = cfg
    block = steps * cols
    z = lax.axis_index("tm")
    sub = lax.axis_index("sub")
    chan = lax.axis_index("chan")
    first = (z * 2 + sub) * steps
    has_low = chan > 0
    has_high = chan < n_chan - 1

    weights = [
        pltpu.make_async_copy(src, dst, w_sem.at[i])
        for i, (src, dst) in enumerate(
            [
                (guess_hbm, guess_ref), (start_hbm, start_ref), (levels_hbm, levels_ref),
                (plan_hbm, plan_ref), (offset_hbm, offset_ref), (w_in_hbm, w_in_raw),
                (te_hbm, te), (w_mid_hbm, w_mid_raw), (w_out_hbm, w_out_raw),
            ]
        )
    ]
    for copy in weights:
        copy.start()

    barrier = pltpu.get_barrier_semaphore()
    next_z = (sub == 1) & (z < n_tm - 1)
    prev_z = (sub == 0) & (z > 0)

    def hello(dev):
        pl.semaphore_signal(barrier, inc=1, device_id=dev, device_id_type=MESH)

    hello({"sub": 1 - sub})
    for k in range(n_tm):
        @pl.when(k != z)
        def _():
            hello({"tm": k})
    @pl.when(next_z)
    def _():
        hello({"tm": z + 1, "sub": 0})
    @pl.when(prev_z)
    def _():
        hello({"tm": z - 1, "sub": 1})
    @pl.when(has_low)
    def _():
        hello({"chan": chan - 1})
    @pl.when(has_high)
    def _():
        hello({"chan": chan + 1})

    weights[0].wait()
    for n in range(steps):
        tile = guess_ref[n].astype(F32)
        for c in range(cols):
            u_scr[pl.ds(n * cols + c, rows, stride=block), :] = tile[:, c * ch:(c + 1) * ch]
    weights[1].wait()
    for c in range(cols):
        st_scr[pl.ds(c, rows, stride=cols), :] = start_ref[:, c * ch:(c + 1) * ch]

    own = (1 + 2 * chan) if two else 3
    n_in = rows + 4 if two else rows + 6
    n1, n2 = n_in - 2, (n_in - 3 if two else n_in - 4)
    o1 = (1 - chan) if two else 0
    if two:
        x1[pl.ds(pl.multiple_of(chan * (n_in - 1) * block, block), block), :] = jnp.zeros((block, 3 * ch), BF16)
        x2[pl.ds(pl.multiple_of(chan * n1 * block, block), block), :] = jnp.zeros((block, 3 * hid), BF16)
        x3[pl.ds(pl.multiple_of(chan * n2 * block, block), block), :] = jnp.zeros((block, 3 * hid), BF16)
    else:
        x1[...] = jnp.zeros(x1.shape, BF16)

    pl.semaphore_wait(
        barrier,
        n_tm + next_z.astype(jnp.int32) + prev_z.astype(jnp.int32)
        + has_low.astype(jnp.int32) + has_high.astype(jnp.int32),
    )

    def halo_copy(sweep, side):
        return pltpu.make_async_remote_copy(
            src_ref=halo_send.at[sweep, side], dst_ref=halo_recv.at[sweep, side],
            send_sem=hs_sem.at[sweep, side], recv_sem=hr_sem.at[sweep, side],
            device_id={"chan": chan - 1 + 2 * side}, device_id_type=MESH,
        )

    def t_copy(sweep, target):
        return pltpu.make_async_remote_copy(
            src_ref=t_send.at[sweep], dst_ref=t_recv.at[sweep, z],
            send_sem=ts_sem.at[sweep, target], recv_sem=tr_sem.at[sweep, z],
            device_id={"tm": target}, device_id_type=MESH,
        )

    def t_arrived(sweep, source):
        return pltpu.make_async_remote_copy(
            src_ref=t_send.at[sweep], dst_ref=t_recv.at[sweep, source],
            send_sem=ts_sem.at[sweep, source], recv_sem=tr_sem.at[sweep, source],
            device_id={"tm": source}, device_id_type=MESH,
        )

    def s_copy(sweep):
        return pltpu.make_async_remote_copy(
            src_ref=s_send.at[sweep], dst_ref=s_recv.at[sweep],
            send_sem=ss_sem.at[sweep], recv_sem=sr_sem.at[sweep],
            device_id={"sub": 1 - sub}, device_id_type=MESH,
        )

    def d_copy(dev):
        return pltpu.make_async_remote_copy(
            src_ref=d_send, dst_ref=d_recv, send_sem=ds_sem, recv_sem=dr_sem,
            device_id=dev, device_id_type=MESH,
        )

    edge = 3 * block

    def send_halo(sweep):
        halo_send[sweep, 0] = fold(u_scr[0:edge, :]).astype(BF16)
        halo_send[sweep, 1] = fold(u_scr[rows * block - edge:rows * block, :]).astype(BF16)
        for side, there in ((0, has_low), (1, has_high)):
            @pl.when(there)
            def _():
                halo_copy(sweep, side).start()

    send_halo(0)

    for i in (2, 3, 4):
        weights[i].wait()
    base = offset_ref[0] + first
    ids = [plan_ref[jnp.minimum(base + n, n_plan - 1)] for n in range(steps + 2)]
    noise = [levels_ref[i] for i in ids]
    size = [noise[n + 1] - noise[n] for n in range(steps + 1)]
    front = [size[n] * jnp.where(first + n == 0, 1.0, 1.5) for n in range(steps)]
    onward = [front[n] - 0.5 * size[n + 1] for n in range(steps)]

    col_of = lax.broadcasted_iota(jnp.int32, (block, 1), 0) % cols

    def spread(value):
        left = jnp.where(col_of == 0, 0.0, pltpu.roll(value, 1, 0))
        right = jnp.where(col_of == cols - 1, 0.0, pltpu.roll(value, block - 1, 0))
        return jnp.concatenate([left, value, right], axis=1).astype(BF16)

    def at(row):
        if isinstance(row, int):
            return pl.ds(row * block, block)
        return pl.ds(pl.multiple_of(row * block, block), block)

    def chosen(n_rows, first_row, r):
        position = chan * rows + first_row + r
        return ((position >= 0) & (position < n_chan * rows)).astype(F32)

    def own_rows():
        for r in range(rows):
            x1[at(own + r), :] = spread(u_scr[r * block:(r + 1) * block, :])

    own_rows()
    weights[5].wait()
    for kr in range(3):
        w_in[kr] = w_in_raw[:, kr * 3 * ch:(kr + 1) * 3 * ch]
    weights[6].wait()
    hot = jnp.zeros((8, n_levels), F32)
    row_of = lax.broadcasted_iota(jnp.int32, (8, n_levels), 0)
    id_of = lax.broadcasted_iota(jnp.int32, (8, n_levels), 1)
    for n in range(steps):
        hot = jnp.where((row_of == n) & (id_of == ids[n]), 1.0, hot)
    embed8 = dot(hot.astype(BF16), te[...])
    embed = jnp.concatenate(
        [jnp.broadcast_to(embed8[n:n + 1], (cols, hid)) for n in range(steps)], axis=0
    )

    for sweep in range(ITERS):
        for side, there in ((1, has_low), (0, has_high)):
            @pl.when(there)
            def _():
                halo_copy(sweep, side).wait_recv()
                got = unfold(halo_recv[sweep, side].astype(F32))
                for r in range(3):
                    x1[at(r if side == 1 else own + rows + r), :] = spread(got[r * block:(r + 1) * block])
        act = dot(x1[0:n1 * block, :], w_in[0])
        for kr in (1, 2):
            act += dot(x1[kr * block:(kr + n1) * block, :], w_in[kr])
        for r in range(n1):
            hidden = silu(act[r * block:(r + 1) * block] + embed)
            if not two:
                hidden = hidden * chosen(n1, -2, r)
            x2[at(o1 + r), :] = spread(hidden)
        if sweep == 0:
            weights[7].wait()
            for kr in range(3):
                w_mid[kr] = w_mid_raw[:, kr * 3 * hid:(kr + 1) * 3 * hid]
        act = dot(x2[0:n2 * block, :], w_mid[0])
        for kr in (1, 2):
            act += dot(x2[kr * block:(kr + n2) * block, :], w_mid[kr])
        for r in range(n2):
            hidden = silu(act[r * block:(r + 1) * block])
            if not two:
                hidden = hidden * chosen(n2, -1, r)
            x3[at(o1 + r), :] = spread(hidden)
        if sweep == 0:
            weights[8].wait()
            for kr in range(3):
                w_sum[kr * ch:(kr + 1) * ch, :] = w_out_raw[:, kr * 3 * hid:(kr + 1) * 3 * hid]
        taps = dot(x3[...], w_sum[...])
        size_out = rows * block
        drift = (
            taps[0:size_out, 0:ch]
            + taps[block:block + size_out, ch:2 * ch]
            + taps[2 * block:2 * block + size_out, 2 * ch:3 * ch]
        ).reshape(rows, steps, cols, ch)

        total = jnp.zeros((rows, cols, ch), F32)
        after = []
        for n in range(steps):
            after.append(total + front[n] * drift[:, n])
            total = total + onward[n] * drift[:, n]
        last = sweep == ITERS - 1
        total = fold(total.reshape(rows * cols, ch))
        t_send[sweep] = total
        for k in range(1, n_tm):
            @pl.when(k > z)
            def _():
                t_copy(sweep, k).start()
        if not last:
            d_send[...] = fold(drift[:, steps - 1].reshape(rows * cols, ch))
            @pl.when(sub == 0)
            def _():
                d_copy({"sub": 1}).start()
            @pl.when(next_z)
            def _():
                d_copy({"tm": z + 1, "sub": 0}).start()
        p_scr[...] = jnp.zeros(p_scr.shape, F32)
        for k in range(n_tm - 1):
            @pl.when(k < z)
            def _():
                t_arrived(sweep, k).wait_recv()
                p_scr[...] += t_recv[sweep, k]
        s_send[sweep] = p_scr[...] + jnp.where(sub == 0, total, 0.0)
        s_copy(sweep).start()
        s_copy(sweep).wait_recv()
        origin = st_scr[...].reshape(rows, cols, ch) + unfold(
            p_scr[...] + s_recv[sweep]
        ).reshape(rows, cols, ch)
        if last:
            for n in range(steps):
                o_scr[n * rows * cols:(n + 1) * rows * cols, :] = (origin + after[n]).reshape(rows * cols, ch)
            for c in range(0, cols, 2):
                out_ref[:, c * ch:(c + 2) * ch] = jnp.concatenate(
                    [o_scr[pl.ds(c + i, steps * rows, stride=cols), :] for i in range(2)], axis=1
                )
        else:
            p_scr[...] = jnp.zeros(p_scr.shape, F32)
            @pl.when((sub == 1) | prev_z)
            def _():
                d_copy({"sub": 1 - sub}).wait_recv()
                p_scr[...] = d_recv[...]
            behind = unfold(p_scr[...]).reshape(rows, cols, ch)
            before = [origin + (0.5 * size[0]) * behind] + [origin + a for a in after[:-1]]
            for r in range(rows):
                for n in range(steps):
                    start = r * block + n * cols
                    u_scr[start:start + cols, :] = before[n][r].astype(BF16).astype(F32)
            send_halo(sweep + 1)
            own_rows()

    for sweep in range(ITERS):
        for side, there in ((0, has_low), (1, has_high)):
            @pl.when(there)
            def _():
                halo_copy(sweep, side).wait_send()
        for k in range(1, n_tm):
            @pl.when(k > z)
            def _():
                t_copy(sweep, k).wait_send()
        s_copy(sweep).wait_send()
    @pl.when((sub == 0) | next_z)
    def _():
        d_copy({"sub": 1 - sub}).wait_send()


def shards(n_chan, n_tm, start_state, guess, w_in, w_mid, w_out, time_embed, levels, plan, offset):
    steps, rows, merged = guess.shape
    ch = w_out.shape[1]
    hid = w_in.shape[1]
    cols = merged // ch
    block = steps * cols
    two = n_chan == 2
    cfg = (steps, rows, cols, ch, hid, n_chan, n_tm, levels.shape[0], plan.shape[0], two)
    n_in = rows + 4 if two else rows + 6
    n_x2 = n_in - 1 if two else n_in - 2
    n_x3 = n_in - 2 if two else n_in - 4
    vmem = pl.BlockSpec(memory_space=pltpu.VMEM)
    hbm = pl.BlockSpec(memory_space=pltpu.HBM)
    dma = pltpu.SemaphoreType.DMA
    half = rows * cols // 2
    out = pl.pallas_call(
        functools.partial(body, cfg),
        out_shape=jax.ShapeDtypeStruct((steps * rows, merged), F32),
        in_specs=[hbm] * 9,
        out_specs=vmem,
        scratch_shapes=[
            pltpu.VMEM(start_state.shape, F32),
            pltpu.VMEM(guess.shape, BF16),
            pltpu.SMEM(levels.shape, F32),
            pltpu.SMEM(plan.shape, jnp.int32),
            pltpu.SMEM(offset.shape, jnp.int32),
            pltpu.VMEM(w_in.shape[::-1], BF16),
            pltpu.VMEM(w_mid.shape[::-1], BF16),
            pltpu.VMEM(w_out.shape[::-1], BF16),
            pltpu.VMEM(time_embed.shape[::-1], BF16),
            pltpu.VMEM((3, hid, 3 * ch), BF16),
            pltpu.VMEM((3, hid, 3 * hid), BF16),
            pltpu.VMEM((3 * ch, 3 * hid), BF16),
            pltpu.VMEM((n_in * block, 3 * ch), BF16),
            pltpu.VMEM((n_x2 * block, 3 * hid), BF16),
            pltpu.VMEM((n_x3 * block, 3 * hid), BF16),
            pltpu.VMEM((rows * block, ch), F32),
            pltpu.VMEM((rows * cols, ch), F32),
            pltpu.VMEM((rows * block, ch), F32),
            pltpu.VMEM((half, 2 * ch), F32),
            pltpu.VMEM((ITERS, 2, 3 * block // 2, 2 * ch), BF16),
            pltpu.VMEM((ITERS, 2, 3 * block // 2, 2 * ch), BF16),
            pltpu.VMEM((ITERS, half, 2 * ch), F32),
            pltpu.VMEM((ITERS, n_tm, half, 2 * ch), F32),
            pltpu.VMEM((ITERS, half, 2 * ch), F32),
            pltpu.VMEM((ITERS, half, 2 * ch), F32),
            pltpu.VMEM((half, 2 * ch), F32),
            pltpu.VMEM((half, 2 * ch), F32),
            dma((9,)),
            dma((ITERS, 2)),
            dma((ITERS, 2)),
            dma((ITERS, n_tm)),
            dma((ITERS, n_tm)),
            dma((ITERS,)),
            dma((ITERS,)),
            dma,
            dma,
        ],
        compiler_params=pltpu.CompilerParams(
            collective_id=0, has_side_effects=True, vmem_limit_bytes=60 * 1024 * 1024
        ),
    )(start_state, guess, levels, plan, offset, w_in.T, w_mid.T, w_out.T, time_embed.T)
    return out.reshape(guess.shape)


def solution(mesh):
    return jax.shard_map(
        functools.partial(shards, mesh.shape["chan"], mesh.shape["tm"]),
        mesh=mesh,
        in_specs=(
            P(("parts", "chan"), None),
            P(("parts", "tm", "sub"), "chan", None),
            P(),
            P(),
            P(),
            P(),
            P(),
            P("parts"),
            P("parts"),
        ),
        out_specs=P(("parts", "tm", "sub"), "chan", None),
        check_vma=False,
    )
```

```python
import functools

import jax
import jax.numpy as jnp
from jax import lax
from jax.experimental import pallas as pl
from jax.experimental.pallas import tpu as pltpu
from jax.sharding import PartitionSpec as P

ITERS = 2
MESH = pl.DeviceIdType.MESH
F32 = jnp.float32
BF16 = jnp.bfloat16


def silu(v):
    half = 0.5 * v
    return half + half * jnp.tanh(half)


def dot(left, right):
    return lax.dot_general(left, right, (((1,), (1,)), ((), ())), preferred_element_type=F32)


def fold(array):
    half = array.shape[0] // 2
    return jnp.concatenate([array[:half], array[half:]], axis=1)


def unfold(array):
    half = array.shape[1] // 2
    return jnp.concatenate([array[:, :half], array[:, half:]], axis=0)


def body(
    cfg,
    start_hbm, guess_hbm, levels_hbm, plan_hbm, offset_hbm, w_in_hbm, w_mid_hbm, w_out_hbm, te_hbm,
    out_ref,
    start_ref, guess_ref, levels_ref, plan_ref, offset_ref,
    w_in_raw, w_mid_raw, w_out_raw, te, w_in, w_mid, w_rest, w_sum, x1, x2, x3, u_scr, st_scr, o_scr, p_scr,
    halo_send, halo_recv, t_send, t_recv, s_send, s_recv, d_send, d_recv,
    w_sem, hs_sem, hr_sem, ts_sem, tr_sem, ss_sem, sr_sem, ds_sem, dr_sem,
):
    steps, rows, cols, ch, hid, n_chan, n_tm, n_levels, n_plan, two = cfg
    block = steps * cols
    n_rest = hid % 128
    z = lax.axis_index("tm")
    sub = lax.axis_index("sub")
    chan = lax.axis_index("chan")
    first = (z * 2 + sub) * steps
    has_low = chan > 0
    has_high = chan < n_chan - 1

    weights = [
        pltpu.make_async_copy(src, dst, w_sem.at[i])
        for i, (src, dst) in enumerate(
            [
                (guess_hbm, guess_ref), (start_hbm, start_ref), (levels_hbm, levels_ref),
                (plan_hbm, plan_ref), (offset_hbm, offset_ref), (w_in_hbm, w_in_raw),
                (te_hbm, te), (w_mid_hbm, w_mid_raw), (w_out_hbm, w_out_raw),
            ]
        )
    ]
    for copy in weights:
        copy.start()

    barrier = pltpu.get_barrier_semaphore()
    next_z = (sub == 1) & (z < n_tm - 1)
    prev_z = (sub == 0) & (z > 0)

    def hello(dev):
        pl.semaphore_signal(barrier, inc=1, device_id=dev, device_id_type=MESH)

    hello({"sub": 1 - sub})
    for k in range(n_tm):
        @pl.when(k != z)
        def _():
            hello({"tm": k})
    @pl.when(next_z)
    def _():
        hello({"tm": z + 1, "sub": 0})
    @pl.when(prev_z)
    def _():
        hello({"tm": z - 1, "sub": 1})
    @pl.when(has_low)
    def _():
        hello({"chan": chan - 1})
    @pl.when(has_high)
    def _():
        hello({"chan": chan + 1})

    weights[0].wait()
    for n in range(steps):
        tile = guess_ref[n].astype(F32)
        for c in range(cols):
            u_scr[pl.ds(n * cols + c, rows, stride=block), :] = tile[:, c * ch:(c + 1) * ch]
    weights[1].wait()
    for c in range(cols):
        st_scr[pl.ds(c, rows, stride=cols), :] = start_ref[:, c * ch:(c + 1) * ch]

    own = (1 + 2 * chan) if two else 3
    n_in = rows + 4 if two else rows + 6
    n1, n2 = n_in - 2, (n_in - 3 if two else n_in - 4)
    o1 = (1 - chan) if two else 0
    if two:
        x1[pl.ds(pl.multiple_of(chan * (n_in - 1) * block, block), block), :] = jnp.zeros((block, 3 * ch), BF16)
        x2[pl.ds(pl.multiple_of(chan * n1 * block, block), block), :] = jnp.zeros((block, 3 * hid), BF16)
        x3[pl.ds(pl.multiple_of(chan * n2 * block, block), block), :] = jnp.zeros((block, 3 * hid), BF16)
    else:
        x1[...] = jnp.zeros(x1.shape, BF16)

    pl.semaphore_wait(
        barrier,
        n_tm + next_z.astype(jnp.int32) + prev_z.astype(jnp.int32)
        + has_low.astype(jnp.int32) + has_high.astype(jnp.int32),
    )

    def halo_copy(sweep, side):
        return pltpu.make_async_remote_copy(
            src_ref=halo_send.at[sweep, side], dst_ref=halo_recv.at[sweep, side],
            send_sem=hs_sem.at[sweep, side], recv_sem=hr_sem.at[sweep, side],
            device_id={"chan": chan - 1 + 2 * side}, device_id_type=MESH,
        )

    def t_copy(sweep, target):
        return pltpu.make_async_remote_copy(
            src_ref=t_send.at[sweep], dst_ref=t_recv.at[sweep, z],
            send_sem=ts_sem.at[sweep, target], recv_sem=tr_sem.at[sweep, z],
            device_id={"tm": target}, device_id_type=MESH,
        )

    def t_arrived(sweep, source):
        return pltpu.make_async_remote_copy(
            src_ref=t_send.at[sweep], dst_ref=t_recv.at[sweep, source],
            send_sem=ts_sem.at[sweep, source], recv_sem=tr_sem.at[sweep, source],
            device_id={"tm": source}, device_id_type=MESH,
        )

    def s_copy(sweep):
        return pltpu.make_async_remote_copy(
            src_ref=s_send.at[sweep], dst_ref=s_recv.at[sweep],
            send_sem=ss_sem.at[sweep], recv_sem=sr_sem.at[sweep],
            device_id={"sub": 1 - sub}, device_id_type=MESH,
        )

    def d_copy(dev):
        return pltpu.make_async_remote_copy(
            src_ref=d_send, dst_ref=d_recv, send_sem=ds_sem, recv_sem=dr_sem,
            device_id=dev, device_id_type=MESH,
        )

    edge = 3 * block

    def send_halo(sweep):
        halo_send[sweep, 0] = fold(u_scr[0:edge, :]).astype(BF16)
        halo_send[sweep, 1] = fold(u_scr[rows * block - edge:rows * block, :]).astype(BF16)
        for side, there in ((0, has_low), (1, has_high)):
            @pl.when(there)
            def _():
                halo_copy(sweep, side).start()

    send_halo(0)

    for i in (2, 3, 4):
        weights[i].wait()
    base = offset_ref[0] + first
    ids = [plan_ref[jnp.minimum(base + n, n_plan - 1)] for n in range(steps + 2)]
    noise = [levels_ref[i] for i in ids]
    size = [noise[n + 1] - noise[n] for n in range(steps + 1)]
    front = [size[n] * jnp.where(first + n == 0, 1.0, 1.5) for n in range(steps)]
    onward = [front[n] - 0.5 * size[n + 1] for n in range(steps)]

    col_of = lax.broadcasted_iota(jnp.int32, (block, 1), 0) % cols

    def spread(value):
        left = jnp.where(col_of == 0, 0.0, pltpu.roll(value, 1, 0))
        right = jnp.where(col_of == cols - 1, 0.0, pltpu.roll(value, block - 1, 0))
        return jnp.concatenate([left, value, right], axis=1).astype(BF16)

    def at(row):
        if isinstance(row, int):
            return pl.ds(row * block, block)
        return pl.ds(pl.multiple_of(row * block, block), block)

    def chosen(n_rows, first_row, r):
        position = chan * rows + first_row + r
        return ((position >= 0) & (position < n_chan * rows)).astype(F32)

    def own_rows():
        for r in range(rows):
            x1[at(own + r), :] = spread(u_scr[r * block:(r + 1) * block, :])

    own_rows()
    weights[5].wait()
    for kr in range(3):
        w_in[kr] = w_in_raw[:, kr * 3 * ch:(kr + 1) * 3 * ch]
    weights[6].wait()
    hot = jnp.zeros((8, n_levels), F32)
    row_of = lax.broadcasted_iota(jnp.int32, (8, n_levels), 0)
    id_of = lax.broadcasted_iota(jnp.int32, (8, n_levels), 1)
    for n in range(steps):
        hot = jnp.where((row_of == n) & (id_of == ids[n]), 1.0, hot)
    embed8 = dot(hot.astype(BF16), te[...])
    embed = jnp.concatenate(
        [jnp.broadcast_to(embed8[n:n + 1], (cols, hid)) for n in range(steps)], axis=0
    )

    weights[7].wait()
    for kr in range(3):
        taps_of = slice(kr * 3 * hid, (kr + 1) * 3 * hid)
        w_mid[kr] = w_mid_raw[0:hid - n_rest, taps_of]
        w_rest[kr * n_rest:(kr + 1) * n_rest, :] = w_mid_raw[hid - n_rest:hid, taps_of]
    weights[8].wait()
    for kr in range(3):
        w_sum[kr * ch:(kr + 1) * ch, :] = w_out_raw[:, kr * 3 * hid:(kr + 1) * 3 * hid]

    for sweep in range(ITERS):
        for side, there in ((1, has_low), (0, has_high)):
            @pl.when(there)
            def _():
                halo_copy(sweep, side).wait_recv()
                got = unfold(halo_recv[sweep, side].astype(F32))
                for r in range(3):
                    x1[at(r if side == 1 else own + rows + r), :] = spread(got[r * block:(r + 1) * block])
        act = dot(x1[0:n1 * block, :], w_in[0])
        for kr in (1, 2):
            act += dot(x1[kr * block:(kr + n1) * block, :], w_in[kr])
        for r in range(n1):
            hidden = silu(act[r * block:(r + 1) * block] + embed)
            if not two:
                hidden = hidden * chosen(n1, -2, r)
            x2[at(o1 + r), :] = spread(hidden)
        main = dot(x2[0:n2 * block, :], w_mid[0])
        for kr in (1, 2):
            main += dot(x2[kr * block:(kr + n2) * block, :], w_mid[kr])
        rest = dot(x2[0:(n2 + 2) * block, :], w_rest[...])
        for r in range(n2):
            tail = sum(
                rest[(r + kr) * block:(r + kr + 1) * block, kr * n_rest:(kr + 1) * n_rest]
                for kr in range(3)
            )
            hidden = silu(jnp.concatenate([main[r * block:(r + 1) * block], tail], axis=1))
            if not two:
                hidden = hidden * chosen(n2, -1, r)
            x3[at(o1 + r), :] = spread(hidden)
        taps = dot(x3[...], w_sum[...])
        size_out = rows * block
        drift = (
            taps[0:size_out, 0:ch]
            + taps[block:block + size_out, ch:2 * ch]
            + taps[2 * block:2 * block + size_out, 2 * ch:3 * ch]
        ).reshape(rows, steps, cols, ch)

        total = jnp.zeros((rows, cols, ch), F32)
        after = []
        for n in range(steps):
            after.append(total + front[n] * drift[:, n])
            total = total + onward[n] * drift[:, n]
        last = sweep == ITERS - 1
        total = fold(total.reshape(rows * cols, ch))
        t_send[sweep] = total.astype(BF16)
        for k in range(1, n_tm):
            @pl.when(k > z)
            def _():
                t_copy(sweep, k).start()
        if not last:
            d_send[...] = fold(drift[:, steps - 1].reshape(rows * cols, ch)).astype(BF16)
            @pl.when(sub == 0)
            def _():
                d_copy({"sub": 1}).start()
            @pl.when(next_z)
            def _():
                d_copy({"tm": z + 1, "sub": 0}).start()
        p_scr[...] = jnp.zeros(p_scr.shape, F32)
        for k in range(n_tm - 1):
            @pl.when(k < z)
            def _():
                t_arrived(sweep, k).wait_recv()
                p_scr[...] += t_recv[sweep, k].astype(F32)
        s_send[sweep] = p_scr[...] + jnp.where(sub == 0, total, 0.0)
        s_copy(sweep).start()
        s_copy(sweep).wait_recv()
        origin = st_scr[...].reshape(rows, cols, ch) + unfold(
            p_scr[...] + s_recv[sweep]
        ).reshape(rows, cols, ch)
        if last:
            for n in range(steps):
                o_scr[n * rows * cols:(n + 1) * rows * cols, :] = (origin + after[n]).reshape(rows * cols, ch)
            for c in range(0, cols, 2):
                pair = jnp.concatenate(
                    [o_scr[pl.ds(c + i, steps * rows, stride=cols), :] for i in range(2)], axis=1
                )
                for n in range(steps):
                    out_ref[n, :, c * ch:(c + 2) * ch] = pair[n * rows:(n + 1) * rows]
        else:
            p_scr[...] = jnp.zeros(p_scr.shape, F32)
            @pl.when((sub == 1) | prev_z)
            def _():
                d_copy({"sub": 1 - sub}).wait_recv()
                p_scr[...] = d_recv[...].astype(F32)
            behind = unfold(p_scr[...]).reshape(rows, cols, ch)
            before = [origin + (0.5 * size[0]) * behind] + [origin + a for a in after[:-1]]
            for r in range(rows):
                for n in range(steps):
                    start = r * block + n * cols
                    u_scr[start:start + cols, :] = before[n][r].astype(BF16).astype(F32)
            send_halo(sweep + 1)
            own_rows()

    for sweep in range(ITERS):
        for side, there in ((0, has_low), (1, has_high)):
            @pl.when(there)
            def _():
                halo_copy(sweep, side).wait_send()
        for k in range(1, n_tm):
            @pl.when(k > z)
            def _():
                t_copy(sweep, k).wait_send()
        s_copy(sweep).wait_send()
    @pl.when((sub == 0) | next_z)
    def _():
        d_copy({"sub": 1 - sub}).wait_send()


def shards(n_chan, n_tm, start_state, guess, w_in, w_mid, w_out, time_embed, levels, plan, offset):
    steps, rows, merged = guess.shape
    ch = w_out.shape[1]
    hid = w_in.shape[1]
    cols = merged // ch
    block = steps * cols
    two = n_chan == 2
    cfg = (steps, rows, cols, ch, hid, n_chan, n_tm, levels.shape[0], plan.shape[0], two)
    n_in = rows + 4 if two else rows + 6
    n_x2 = n_in - 1 if two else n_in - 2
    n_x3 = n_in - 2 if two else n_in - 4
    vmem = pl.BlockSpec(memory_space=pltpu.VMEM)
    hbm = pl.BlockSpec(memory_space=pltpu.HBM)
    dma = pltpu.SemaphoreType.DMA
    half = rows * cols // 2
    out = pl.pallas_call(
        functools.partial(body, cfg),
        out_shape=jax.ShapeDtypeStruct(guess.shape, F32),
        in_specs=[hbm] * 9,
        out_specs=vmem,
        scratch_shapes=[
            pltpu.VMEM(start_state.shape, F32),
            pltpu.VMEM(guess.shape, BF16),
            pltpu.SMEM(levels.shape, F32),
            pltpu.SMEM(plan.shape, jnp.int32),
            pltpu.SMEM(offset.shape, jnp.int32),
            pltpu.VMEM(w_in.shape[::-1], BF16),
            pltpu.VMEM(w_mid.shape[::-1], BF16),
            pltpu.VMEM(w_out.shape[::-1], BF16),
            pltpu.VMEM(time_embed.shape[::-1], BF16),
            pltpu.VMEM((3, hid, 3 * ch), BF16),
            pltpu.VMEM((3, hid - hid % 128, 3 * hid), BF16),
            pltpu.VMEM((3 * (hid % 128), 3 * hid), BF16),
            pltpu.VMEM((3 * ch, 3 * hid), BF16),
            pltpu.VMEM((n_in * block, 3 * ch), BF16),
            pltpu.VMEM((n_x2 * block, 3 * hid), BF16),
            pltpu.VMEM((n_x3 * block, 3 * hid), BF16),
            pltpu.VMEM((rows * block, ch), F32),
            pltpu.VMEM((rows * cols, ch), F32),
            pltpu.VMEM((rows * block, ch), F32),
            pltpu.VMEM((half, 2 * ch), F32),
            pltpu.VMEM((ITERS, 2, 3 * block // 2, 2 * ch), BF16),
            pltpu.VMEM((ITERS, 2, 3 * block // 2, 2 * ch), BF16),
            pltpu.VMEM((ITERS, half, 2 * ch), BF16),
            pltpu.VMEM((ITERS, n_tm, half, 2 * ch), BF16),
            pltpu.VMEM((ITERS, half, 2 * ch), F32),
            pltpu.VMEM((ITERS, half, 2 * ch), F32),
            pltpu.VMEM((half, 2 * ch), BF16),
            pltpu.VMEM((half, 2 * ch), BF16),
            dma((9,)),
            dma((ITERS, 2)),
            dma((ITERS, 2)),
            dma((ITERS, n_tm)),
            dma((ITERS, n_tm)),
            dma((ITERS,)),
            dma((ITERS,)),
            dma,
            dma,
        ],
        compiler_params=pltpu.CompilerParams(
            collective_id=0, has_side_effects=True, vmem_limit_bytes=60 * 1024 * 1024
        ),
    )(start_state, guess, levels, plan, offset, w_in.T, w_mid.T, w_out.T, time_embed.T)
    return out


def solution(mesh):
    return jax.shard_map(
        functools.partial(shards, mesh.shape["chan"], mesh.shape["tm"]),
        mesh=mesh,
        in_specs=(
            P(("parts", "chan"), None),
            P(("parts", "tm", "sub"), "chan", None),
            P(),
            P(),
            P(),
            P(),
            P(),
            P("parts"),
            P("parts"),
        ),
        out_specs=P(("parts", "tm", "sub"), "chan", None),
        check_vma=False,
    )
```

```python
import functools

import jax
import jax.numpy as jnp
from jax import lax
from jax.experimental import pallas as pl
from jax.experimental.pallas import tpu as pltpu
from jax.sharding import PartitionSpec as P

ITERS = 2
MESH = pl.DeviceIdType.MESH
F32 = jnp.float32
BF16 = jnp.bfloat16


def silu(v):
    half = 0.5 * v
    return half + half * jnp.tanh(half)


def dot(left, right):
    return lax.dot_general(left, right, (((1,), (1,)), ((), ())), preferred_element_type=F32)


def fold(array):
    half = array.shape[0] // 2
    return jnp.concatenate([array[:half], array[half:]], axis=1)


def unfold(array):
    half = array.shape[1] // 2
    return jnp.concatenate([array[:, :half], array[:, half:]], axis=0)


def body(
    cfg,
    start_hbm, guess_hbm, levels_hbm, plan_hbm, offset_hbm, w_in_hbm, w_mid_hbm, w_out_hbm, te_hbm,
    out_ref,
    start_ref, guess_ref, levels_ref, plan_ref, offset_ref,
    w_in_raw, w_mid_raw, w_out_raw, te, w_in, w_mid, w_rest, w_sum, x1, x2, x3, u_scr, st_scr, o_scr, p_scr,
    halo_send, halo_recv, t_send, t_recv, s_send, s_recv, d_send, d_recv,
    w_sem, hs_sem, hr_sem, ts_sem, tr_sem, ss_sem, sr_sem, ds_sem, dr_sem,
):
    steps, rows, cols, ch, hid, n_chan, n_tm, n_levels, n_plan, two = cfg
    block = steps * cols
    n_rest = hid % 128
    z = lax.axis_index("tm")
    sub = lax.axis_index("sub")
    chan = lax.axis_index("chan")
    first = (z * 2 + sub) * steps
    has_low = chan > 0
    has_high = chan < n_chan - 1

    weights = [
        pltpu.make_async_copy(src, dst, w_sem.at[i])
        for i, (src, dst) in enumerate(
            [
                (guess_hbm, guess_ref), (start_hbm, start_ref), (levels_hbm, levels_ref),
                (plan_hbm, plan_ref), (offset_hbm, offset_ref), (w_in_hbm, w_in_raw),
                (te_hbm, te), (w_mid_hbm, w_mid_raw), (w_out_hbm, w_out_raw),
            ]
        )
    ]
    for copy in weights:
        copy.start()

    barrier = pltpu.get_barrier_semaphore()
    next_z = (sub == 1) & (z < n_tm - 1)
    prev_z = (sub == 0) & (z > 0)

    def hello(dev):
        pl.semaphore_signal(barrier, inc=1, device_id=dev, device_id_type=MESH)

    hello({"sub": 1 - sub})
    for k in range(n_tm):
        @pl.when(k != z)
        def _():
            hello({"tm": k})
    @pl.when(next_z)
    def _():
        hello({"tm": z + 1, "sub": 0})
    @pl.when(prev_z)
    def _():
        hello({"tm": z - 1, "sub": 1})
    @pl.when(has_low)
    def _():
        hello({"chan": chan - 1})
    @pl.when(has_high)
    def _():
        hello({"chan": chan + 1})

    weights[0].wait()
    for n in range(steps):
        tile = guess_ref[n].astype(F32)
        for c in range(cols):
            u_scr[pl.ds(n * cols + c, rows, stride=block), :] = tile[:, c * ch:(c + 1) * ch]
    weights[1].wait()
    for c in range(cols):
        st_scr[pl.ds(c, rows, stride=cols), :] = start_ref[:, c * ch:(c + 1) * ch]

    own = (1 + 2 * chan) if two else 3
    n_in = rows + 4 if two else rows + 6
    n1, n2 = n_in - 2, (n_in - 3 if two else n_in - 4)
    o1 = (1 - chan) if two else 0
    if two:
        x1[pl.ds(pl.multiple_of(chan * (n_in - 1) * block, block), block), :] = jnp.zeros((block, 3 * ch), BF16)
        x2[pl.ds(pl.multiple_of(chan * n1 * block, block), block), :] = jnp.zeros((block, 3 * hid), BF16)
        x3[pl.ds(pl.multiple_of(chan * n2 * block, block), block), :] = jnp.zeros((block, 3 * hid), BF16)
    else:
        x1[...] = jnp.zeros(x1.shape, BF16)

    pl.semaphore_wait(
        barrier,
        n_tm + next_z.astype(jnp.int32) + prev_z.astype(jnp.int32)
        + has_low.astype(jnp.int32) + has_high.astype(jnp.int32),
    )

    def halo_copy(sweep, side):
        return pltpu.make_async_remote_copy(
            src_ref=halo_send.at[sweep, side], dst_ref=halo_recv.at[sweep, side],
            send_sem=hs_sem.at[sweep, side], recv_sem=hr_sem.at[sweep, side],
            device_id={"chan": chan - 1 + 2 * side}, device_id_type=MESH,
        )

    def t_copy(sweep, target):
        return pltpu.make_async_remote_copy(
            src_ref=t_send.at[sweep], dst_ref=t_recv.at[sweep, z],
            send_sem=ts_sem.at[sweep, target], recv_sem=tr_sem.at[sweep, z],
            device_id={"tm": target}, device_id_type=MESH,
        )

    def t_arrived(sweep, source):
        return pltpu.make_async_remote_copy(
            src_ref=t_send.at[sweep], dst_ref=t_recv.at[sweep, source],
            send_sem=ts_sem.at[sweep, source], recv_sem=tr_sem.at[sweep, source],
            device_id={"tm": source}, device_id_type=MESH,
        )

    def s_copy(sweep):
        return pltpu.make_async_remote_copy(
            src_ref=s_send.at[sweep], dst_ref=s_recv.at[sweep],
            send_sem=ss_sem.at[sweep], recv_sem=sr_sem.at[sweep],
            device_id={"sub": 1 - sub}, device_id_type=MESH,
        )

    def d_copy(dev):
        return pltpu.make_async_remote_copy(
            src_ref=d_send, dst_ref=d_recv, send_sem=ds_sem, recv_sem=dr_sem,
            device_id=dev, device_id_type=MESH,
        )

    edge = 3 * block

    def send_halo(sweep):
        halo_send[sweep, 0] = fold(u_scr[0:edge, :]).astype(BF16)
        halo_send[sweep, 1] = fold(u_scr[rows * block - edge:rows * block, :]).astype(BF16)
        for side, there in ((0, has_low), (1, has_high)):
            @pl.when(there)
            def _():
                halo_copy(sweep, side).start()

    send_halo(0)

    for i in (2, 3, 4):
        weights[i].wait()
    base = offset_ref[0] + first
    ids = [plan_ref[jnp.minimum(base + n, n_plan - 1)] for n in range(steps + 2)]
    noise = [levels_ref[i] for i in ids]
    size = [noise[n + 1] - noise[n] for n in range(steps + 1)]
    front = [size[n] * jnp.where(first + n == 0, 1.0, 1.5) for n in range(steps)]
    onward = [front[n] - 0.5 * size[n + 1] for n in range(steps)]

    col_of = lax.broadcasted_iota(jnp.int32, (block, 1), 0) % cols

    def spread(value):
        left = jnp.where(col_of == 0, 0.0, pltpu.roll(value, 1, 0))
        right = jnp.where(col_of == cols - 1, 0.0, pltpu.roll(value, block - 1, 0))
        return jnp.concatenate([left, value, right], axis=1).astype(BF16)

    def at(row):
        if isinstance(row, int):
            return pl.ds(row * block, block)
        return pl.ds(pl.multiple_of(row * block, block), block)

    def chosen(n_rows, first_row, r):
        position = chan * rows + first_row + r
        return ((position >= 0) & (position < n_chan * rows)).astype(F32)

    def own_rows():
        for r in range(rows):
            x1[at(own + r), :] = spread(u_scr[r * block:(r + 1) * block, :])

    own_rows()
    weights[5].wait()
    for kr in range(3):
        w_in[kr] = w_in_raw[:, kr * 3 * ch:(kr + 1) * 3 * ch]
    weights[6].wait()
    hot = jnp.zeros((8, n_levels), F32)
    row_of = lax.broadcasted_iota(jnp.int32, (8, n_levels), 0)
    id_of = lax.broadcasted_iota(jnp.int32, (8, n_levels), 1)
    for n in range(steps):
        hot = jnp.where((row_of == n) & (id_of == ids[n]), 1.0, hot)
    embed8 = dot(hot.astype(BF16), te[...])
    embed = jnp.concatenate(
        [jnp.broadcast_to(embed8[n:n + 1], (cols, hid)) for n in range(steps)], axis=0
    )

    weights[7].wait()
    for kr in range(3):
        taps_of = slice(kr * 3 * hid, (kr + 1) * 3 * hid)
        w_mid[kr] = w_mid_raw[0:hid - n_rest, taps_of]
        w_rest[kr * n_rest:(kr + 1) * n_rest, :] = w_mid_raw[hid - n_rest:hid, taps_of]
    weights[8].wait()
    for kr in range(3):
        w_sum[kr * ch:(kr + 1) * ch, :] = w_out_raw[:, kr * 3 * hid:(kr + 1) * 3 * hid]

    def first_layer(start, count):
        def taps(kr):
            return x1[pl.ds((start + kr) * block if isinstance(start, int) else pl.multiple_of((start + kr) * block, block), count * block), :]

        act = dot(taps(0), w_in[0]) + dot(taps(1), w_in[1]) + dot(taps(2), w_in[2])
        for r in range(count):
            hidden = silu(act[r * block:(r + 1) * block] + embed)
            if not two:
                hidden = hidden * chosen(n1, -2, r)
            x2[at(o1 + start + r), :] = spread(hidden)

    for sweep in range(ITERS):
        if two:
            first_layer(3 * chan, n1 // 2)
        for side, there in ((1, has_low), (0, has_high)):
            @pl.when(there)
            def _():
                halo_copy(sweep, side).wait_recv()
                got = unfold(halo_recv[sweep, side].astype(F32))
                for r in range(3):
                    x1[at(r if side == 1 else own + rows + r), :] = spread(got[r * block:(r + 1) * block])
        first_layer(3 * (1 - chan) if two else 0, n1 // 2 if two else n1)
        main = dot(x2[0:n2 * block, :], w_mid[0])
        for kr in (1, 2):
            main += dot(x2[kr * block:(kr + n2) * block, :], w_mid[kr])
        rest = dot(x2[0:(n2 + 2) * block, :], w_rest[...])
        for r in range(n2):
            tail = sum(
                rest[(r + kr) * block:(r + kr + 1) * block, kr * n_rest:(kr + 1) * n_rest]
                for kr in range(3)
            )
            hidden = silu(jnp.concatenate([main[r * block:(r + 1) * block], tail], axis=1))
            if not two:
                hidden = hidden * chosen(n2, -1, r)
            x3[at(o1 + r), :] = spread(hidden)
        taps = dot(x3[...], w_sum[...])
        size_out = rows * block
        drift = (
            taps[0:size_out, 0:ch]
            + taps[block:block + size_out, ch:2 * ch]
            + taps[2 * block:2 * block + size_out, 2 * ch:3 * ch]
        ).reshape(rows, steps, cols, ch)

        total = jnp.zeros((rows, cols, ch), F32)
        after = []
        for n in range(steps):
            after.append(total + front[n] * drift[:, n])
            total = total + onward[n] * drift[:, n]
        last = sweep == ITERS - 1
        total = fold(total.reshape(rows * cols, ch))
        t_send[sweep] = total.astype(BF16)
        for k in range(n_tm - 1, 0, -1):
            @pl.when(k > z)
            def _():
                t_copy(sweep, k).start()
        if not last:
            d_send[...] = fold(drift[:, steps - 1].reshape(rows * cols, ch)).astype(BF16)
            @pl.when(sub == 0)
            def _():
                d_copy({"sub": 1}).start()
            @pl.when(next_z)
            def _():
                d_copy({"tm": z + 1, "sub": 0}).start()
        p_scr[...] = jnp.zeros(p_scr.shape, F32)
        for k in range(n_tm - 1):
            @pl.when(k < z)
            def _():
                t_arrived(sweep, k).wait_recv()
                p_scr[...] += t_recv[sweep, k].astype(F32)
        s_send[sweep] = p_scr[...] + jnp.where(sub == 0, total, 0.0)
        s_copy(sweep).start()
        s_copy(sweep).wait_recv()
        origin = st_scr[...].reshape(rows, cols, ch) + unfold(
            p_scr[...] + s_recv[sweep]
        ).reshape(rows, cols, ch)
        if last:
            for n in range(steps):
                o_scr[n * rows * cols:(n + 1) * rows * cols, :] = (origin + after[n]).reshape(rows * cols, ch)
            for c in range(0, cols, 2):
                pair = jnp.concatenate(
                    [o_scr[pl.ds(c + i, steps * rows, stride=cols), :] for i in range(2)], axis=1
                )
                for n in range(steps):
                    out_ref[n, :, c * ch:(c + 2) * ch] = pair[n * rows:(n + 1) * rows]
        else:
            p_scr[...] = jnp.zeros(p_scr.shape, F32)
            @pl.when((sub == 1) | prev_z)
            def _():
                d_copy({"sub": 1 - sub}).wait_recv()
                p_scr[...] = d_recv[...].astype(F32)
            behind = unfold(p_scr[...]).reshape(rows, cols, ch)
            before = [origin + (0.5 * size[0]) * behind] + [origin + a for a in after[:-1]]
            for r in range(rows):
                for n in range(steps):
                    start = r * block + n * cols
                    u_scr[start:start + cols, :] = before[n][r].astype(BF16).astype(F32)
            send_halo(sweep + 1)
            own_rows()

    for sweep in range(ITERS):
        for side, there in ((0, has_low), (1, has_high)):
            @pl.when(there)
            def _():
                halo_copy(sweep, side).wait_send()
        for k in range(1, n_tm):
            @pl.when(k > z)
            def _():
                t_copy(sweep, k).wait_send()
        s_copy(sweep).wait_send()
    @pl.when((sub == 0) | next_z)
    def _():
        d_copy({"sub": 1 - sub}).wait_send()


def shards(n_chan, n_tm, start_state, guess, w_in, w_mid, w_out, time_embed, levels, plan, offset):
    steps, rows, merged = guess.shape
    ch = w_out.shape[1]
    hid = w_in.shape[1]
    cols = merged // ch
    block = steps * cols
    two = n_chan == 2 and rows == 4
    cfg = (steps, rows, cols, ch, hid, n_chan, n_tm, levels.shape[0], plan.shape[0], two)
    n_in = rows + 4 if two else rows + 6
    n_x2 = n_in - 1 if two else n_in - 2
    n_x3 = n_in - 2 if two else n_in - 4
    vmem = pl.BlockSpec(memory_space=pltpu.VMEM)
    hbm = pl.BlockSpec(memory_space=pltpu.HBM)
    dma = pltpu.SemaphoreType.DMA
    half = rows * cols // 2
    out = pl.pallas_call(
        functools.partial(body, cfg),
        out_shape=jax.ShapeDtypeStruct(guess.shape, F32),
        in_specs=[hbm] * 9,
        out_specs=vmem,
        scratch_shapes=[
            pltpu.VMEM(start_state.shape, F32),
            pltpu.VMEM(guess.shape, BF16),
            pltpu.SMEM(levels.shape, F32),
            pltpu.SMEM(plan.shape, jnp.int32),
            pltpu.SMEM(offset.shape, jnp.int32),
            pltpu.VMEM(w_in.shape[::-1], BF16),
            pltpu.VMEM(w_mid.shape[::-1], BF16),
            pltpu.VMEM(w_out.shape[::-1], BF16),
            pltpu.VMEM(time_embed.shape[::-1], BF16),
            pltpu.VMEM((3, hid, 3 * ch), BF16),
            pltpu.VMEM((3, hid - hid % 128, 3 * hid), BF16),
            pltpu.VMEM((3 * (hid % 128), 3 * hid), BF16),
            pltpu.VMEM((3 * ch, 3 * hid), BF16),
            pltpu.VMEM((n_in * block, 3 * ch), BF16),
            pltpu.VMEM((n_x2 * block, 3 * hid), BF16),
            pltpu.VMEM((n_x3 * block, 3 * hid), BF16),
            pltpu.VMEM((rows * block, ch), F32),
            pltpu.VMEM((rows * cols, ch), F32),
            pltpu.VMEM((rows * block, ch), F32),
            pltpu.VMEM((half, 2 * ch), F32),
            pltpu.VMEM((ITERS, 2, 3 * block // 2, 2 * ch), BF16),
            pltpu.VMEM((ITERS, 2, 3 * block // 2, 2 * ch), BF16),
            pltpu.VMEM((ITERS, half, 2 * ch), BF16),
            pltpu.VMEM((ITERS, n_tm, half, 2 * ch), BF16),
            pltpu.VMEM((ITERS, half, 2 * ch), F32),
            pltpu.VMEM((ITERS, half, 2 * ch), F32),
            pltpu.VMEM((half, 2 * ch), BF16),
            pltpu.VMEM((half, 2 * ch), BF16),
            dma((9,)),
            dma((ITERS, 2)),
            dma((ITERS, 2)),
            dma((ITERS, n_tm)),
            dma((ITERS, n_tm)),
            dma((ITERS,)),
            dma((ITERS,)),
            dma,
            dma,
        ],
        compiler_params=pltpu.CompilerParams(
            collective_id=0, has_side_effects=True, vmem_limit_bytes=60 * 1024 * 1024
        ),
    )(start_state, guess, levels, plan, offset, w_in.T, w_mid.T, w_out.T, time_embed.T)
    return out


def solution(mesh):
    return jax.shard_map(
        functools.partial(shards, mesh.shape["chan"], mesh.shape["tm"]),
        mesh=mesh,
        in_specs=(
            P(("parts", "chan"), None),
            P(("parts", "tm", "sub"), "chan", None),
            P(),
            P(),
            P(),
            P(),
            P(),
            P("parts"),
            P("parts"),
        ),
        out_specs=P(("parts", "tm", "sub"), "chan", None),
        check_vma=False,
    )
```

```python
import functools

import jax
import jax.numpy as jnp
from jax import lax
from jax.experimental import pallas as pl
from jax.experimental.pallas import tpu as pltpu
from jax.sharding import PartitionSpec as P

ITERS = 2
MESH = pl.DeviceIdType.MESH
F32 = jnp.float32
BF16 = jnp.bfloat16


def silu(v):
    half = 0.5 * v
    return half + half * jnp.tanh(half)


def dot(left, right):
    return lax.dot_general(left, right, (((1,), (1,)), ((), ())), preferred_element_type=F32)


def fold(array):
    half = array.shape[0] // 2
    return jnp.concatenate([array[:half], array[half:]], axis=1)


def unfold(array):
    half = array.shape[1] // 2
    return jnp.concatenate([array[:, :half], array[:, half:]], axis=0)


def body(
    cfg,
    start_hbm, guess_hbm, levels_hbm, plan_hbm, offset_hbm, w_in_hbm, w_mid_hbm, w_out_hbm, te_hbm,
    out_ref,
    start_ref, guess_ref, levels_ref, plan_ref, offset_ref,
    w_in_raw, w_mid_raw, w_out_raw, te, w_in, w_mid, w_rest, w_sum, x1, x2, x3, u_scr, st_scr, o_scr, p_scr,
    halo_send, halo_recv, t_send, t_recv, s_send, s_recv, d_send, d_recv,
    w_sem, hs_sem, hr_sem, ts_sem, tr_sem, ss_sem, sr_sem, ds_sem, dr_sem,
):
    steps, rows, cols, ch, hid, n_chan, n_tm, n_levels, n_plan, two = cfg
    block = steps * cols
    n_rest = hid % 128
    z = lax.axis_index("tm")
    sub = lax.axis_index("sub")
    chan = lax.axis_index("chan")
    first = (z * 2 + sub) * steps
    has_low = chan > 0
    has_high = chan < n_chan - 1

    weights = [
        pltpu.make_async_copy(src, dst, w_sem.at[i])
        for i, (src, dst) in enumerate(
            [
                (guess_hbm, guess_ref), (start_hbm, start_ref), (levels_hbm, levels_ref),
                (plan_hbm, plan_ref), (offset_hbm, offset_ref), (w_in_hbm, w_in_raw),
                (te_hbm, te), (w_mid_hbm, w_mid_raw), (w_out_hbm, w_out_raw),
            ]
        )
    ]
    for copy in weights:
        copy.start()

    barrier = pltpu.get_barrier_semaphore()
    next_z = (sub == 1) & (z < n_tm - 1)
    prev_z = (sub == 0) & (z > 0)

    def hello(dev):
        pl.semaphore_signal(barrier, inc=1, device_id=dev, device_id_type=MESH)

    hello({"sub": 1 - sub})
    for k in range(n_tm):
        @pl.when(k != z)
        def _():
            hello({"tm": k})
    @pl.when(next_z)
    def _():
        hello({"tm": z + 1, "sub": 0})
    @pl.when(prev_z)
    def _():
        hello({"tm": z - 1, "sub": 1})
    @pl.when(has_low)
    def _():
        hello({"chan": chan - 1})
    @pl.when(has_high)
    def _():
        hello({"chan": chan + 1})

    weights[0].wait()
    for n in range(steps):
        tile = guess_ref[n].astype(F32)
        for c in range(cols):
            u_scr[pl.ds(n * cols + c, rows, stride=block), :] = tile[:, c * ch:(c + 1) * ch]
    weights[1].wait()
    for c in range(cols):
        st_scr[pl.ds(c, rows, stride=cols), :] = start_ref[:, c * ch:(c + 1) * ch]

    own = (1 + 2 * chan) if two else 3
    n_in = rows + 4 if two else rows + 6
    n1, n2 = n_in - 2, (n_in - 3 if two else n_in - 4)
    o1 = (1 - chan) if two else 0
    if two:
        x1[pl.ds(pl.multiple_of(chan * (n_in - 1) * block, block), block), :] = jnp.zeros((block, 3 * ch), BF16)
        x2[pl.ds(pl.multiple_of(chan * n1 * block, block), block), :] = jnp.zeros((block, 3 * hid), BF16)
        x3[pl.ds(pl.multiple_of(chan * n2 * block, block), block), :] = jnp.zeros((block, 3 * hid), BF16)
    else:
        x1[...] = jnp.zeros(x1.shape, BF16)

    pl.semaphore_wait(
        barrier,
        n_tm + next_z.astype(jnp.int32) + prev_z.astype(jnp.int32)
        + has_low.astype(jnp.int32) + has_high.astype(jnp.int32),
    )

    def halo_copy(sweep, side):
        return pltpu.make_async_remote_copy(
            src_ref=halo_send.at[sweep, side], dst_ref=halo_recv.at[sweep, side],
            send_sem=hs_sem.at[sweep, side], recv_sem=hr_sem.at[sweep, side],
            device_id={"chan": chan - 1 + 2 * side}, device_id_type=MESH,
        )

    def t_copy(sweep, target):
        return pltpu.make_async_remote_copy(
            src_ref=t_send.at[sweep], dst_ref=t_recv.at[sweep, z],
            send_sem=ts_sem.at[sweep, target], recv_sem=tr_sem.at[sweep, z],
            device_id={"tm": target}, device_id_type=MESH,
        )

    def t_arrived(sweep, source):
        return pltpu.make_async_remote_copy(
            src_ref=t_send.at[sweep], dst_ref=t_recv.at[sweep, source],
            send_sem=ts_sem.at[sweep, source], recv_sem=tr_sem.at[sweep, source],
            device_id={"tm": source}, device_id_type=MESH,
        )

    def s_copy(sweep):
        return pltpu.make_async_remote_copy(
            src_ref=s_send.at[sweep], dst_ref=s_recv.at[sweep],
            send_sem=ss_sem.at[sweep], recv_sem=sr_sem.at[sweep],
            device_id={"sub": 1 - sub}, device_id_type=MESH,
        )

    def d_copy(dev):
        return pltpu.make_async_remote_copy(
            src_ref=d_send, dst_ref=d_recv, send_sem=ds_sem, recv_sem=dr_sem,
            device_id=dev, device_id_type=MESH,
        )

    edge = 3 * block

    def send_halo(sweep):
        halo_send[sweep, 0] = fold(u_scr[0:edge, :]).astype(BF16)
        halo_send[sweep, 1] = fold(u_scr[rows * block - edge:rows * block, :]).astype(BF16)
        for side, there in ((0, has_low), (1, has_high)):
            @pl.when(there)
            def _():
                halo_copy(sweep, side).start()

    send_halo(0)

    for i in (2, 3, 4):
        weights[i].wait()
    base = offset_ref[0] + first
    ids = [plan_ref[jnp.minimum(base + n, n_plan - 1)] for n in range(steps + 2)]
    noise = [levels_ref[i] for i in ids]
    size = [noise[n + 1] - noise[n] for n in range(steps + 1)]
    front = [size[n] * jnp.where(first + n == 0, 1.0, 1.5) for n in range(steps)]
    onward = [front[n] - 0.5 * size[n + 1] for n in range(steps)]

    col_of = lax.broadcasted_iota(jnp.int32, (block, 1), 0) % cols

    def spread(value):
        left = jnp.where(col_of == 0, 0.0, pltpu.roll(value, 1, 0))
        right = jnp.where(col_of == cols - 1, 0.0, pltpu.roll(value, block - 1, 0))
        return jnp.concatenate([left, value, right], axis=1).astype(BF16)

    def at(row):
        if isinstance(row, int):
            return pl.ds(row * block, block)
        return pl.ds(pl.multiple_of(row * block, block), block)

    def chosen(n_rows, first_row, r):
        position = chan * rows + first_row + r
        return ((position >= 0) & (position < n_chan * rows)).astype(F32)

    def own_rows():
        for r in range(rows):
            x1[at(own + r), :] = spread(u_scr[r * block:(r + 1) * block, :])

    own_rows()
    weights[5].wait()
    for kr in range(3):
        w_in[kr] = w_in_raw[:, kr * 3 * ch:(kr + 1) * 3 * ch]
    weights[6].wait()
    hot = jnp.zeros((8, n_levels), F32)
    row_of = lax.broadcasted_iota(jnp.int32, (8, n_levels), 0)
    id_of = lax.broadcasted_iota(jnp.int32, (8, n_levels), 1)
    for n in range(steps):
        hot = jnp.where((row_of == n) & (id_of == ids[n]), 1.0, hot)
    embed8 = dot(hot.astype(BF16), te[...])
    embed = jnp.concatenate(
        [jnp.broadcast_to(embed8[n:n + 1], (cols, hid)) for n in range(steps)], axis=0
    )

    weights[7].wait()
    for kr in range(3):
        taps_of = slice(kr * 3 * hid, (kr + 1) * 3 * hid)
        w_mid[kr] = w_mid_raw[0:hid - n_rest, taps_of]
        w_rest[kr * n_rest:(kr + 1) * n_rest, :] = w_mid_raw[hid - n_rest:hid, taps_of]
    weights[8].wait()
    for kr in range(3):
        w_sum[kr * ch:(kr + 1) * ch, :] = w_out_raw[:, kr * 3 * hid:(kr + 1) * 3 * hid]

    def first_layer(start, count):
        def taps(kr):
            return x1[pl.ds((start + kr) * block if isinstance(start, int) else pl.multiple_of((start + kr) * block, block), count * block), :]

        act = dot(taps(0), w_in[0]) + dot(taps(1), w_in[1]) + dot(taps(2), w_in[2])
        for r in range(count):
            hidden = silu(act[r * block:(r + 1) * block] + embed)
            if not two:
                hidden = hidden * chosen(n1, -2, r)
            x2[at(o1 + start + r), :] = spread(hidden)

    for sweep in range(ITERS):
        if two:
            first_layer(3 * chan, n1 // 2)
        for side, there in ((1, has_low), (0, has_high)):
            @pl.when(there)
            def _():
                halo_copy(sweep, side).wait_recv()
                got = unfold(halo_recv[sweep, side].astype(F32))
                for r in range(3):
                    x1[at(r if side == 1 else own + rows + r), :] = spread(got[r * block:(r + 1) * block])
        first_layer(3 * (1 - chan) if two else 0, n1 // 2 if two else n1)
        main = dot(x2[0:n2 * block, :], w_mid[0])
        for kr in (1, 2):
            main += dot(x2[kr * block:(kr + n2) * block, :], w_mid[kr])
        rest = dot(x2[0:(n2 + 2) * block, :], w_rest[...])
        for r in range(n2):
            tail = sum(
                rest[(r + kr) * block:(r + kr + 1) * block, kr * n_rest:(kr + 1) * n_rest]
                for kr in range(3)
            )
            hidden = silu(jnp.concatenate([main[r * block:(r + 1) * block], tail], axis=1))
            if not two:
                hidden = hidden * chosen(n2, -1, r)
            x3[at(o1 + r), :] = spread(hidden)
        taps = dot(x3[...], w_sum[...])
        size_out = rows * block
        drift = (
            taps[0:size_out, 0:ch]
            + taps[block:block + size_out, ch:2 * ch]
            + taps[2 * block:2 * block + size_out, 2 * ch:3 * ch]
        ).reshape(rows, steps, cols, ch)

        total = jnp.zeros((rows, cols, ch), F32)
        for n in range(steps):
            total = total + onward[n] * drift[:, n]
        last = sweep == ITERS - 1
        total = fold(total.reshape(rows * cols, ch))
        t_send[sweep] = total.astype(BF16)
        for k in range(n_tm - 1, 0, -1):
            @pl.when(k > z)
            def _():
                t_copy(sweep, k).start()
        if not last:
            d_send[...] = fold(drift[:, steps - 1].reshape(rows * cols, ch)).astype(BF16)
            @pl.when(sub == 0)
            def _():
                d_copy({"sub": 1}).start()
            @pl.when(next_z)
            def _():
                d_copy({"tm": z + 1, "sub": 0}).start()
        running = jnp.zeros((rows, cols, ch), F32)
        after = []
        for n in range(steps):
            after.append(running + front[n] * drift[:, n])
            running = running + onward[n] * drift[:, n]
        p_scr[...] = jnp.zeros(p_scr.shape, F32)
        for k in range(n_tm - 1):
            @pl.when(k < z)
            def _():
                t_arrived(sweep, k).wait_recv()
                p_scr[...] += t_recv[sweep, k].astype(F32)
        s_send[sweep] = p_scr[...] + jnp.where(sub == 0, total, 0.0)
        s_copy(sweep).start()
        s_copy(sweep).wait_recv()
        origin = st_scr[...].reshape(rows, cols, ch) + unfold(
            p_scr[...] + s_recv[sweep]
        ).reshape(rows, cols, ch)
        if last:
            for n in range(steps):
                o_scr[n * rows * cols:(n + 1) * rows * cols, :] = (origin + after[n]).reshape(rows * cols, ch)
            for c in range(0, cols, 2):
                pair = jnp.concatenate(
                    [o_scr[pl.ds(c + i, steps * rows, stride=cols), :] for i in range(2)], axis=1
                )
                for n in range(steps):
                    out_ref[n, :, c * ch:(c + 2) * ch] = pair[n * rows:(n + 1) * rows]
        else:
            p_scr[...] = jnp.zeros(p_scr.shape, F32)
            @pl.when((sub == 1) | prev_z)
            def _():
                d_copy({"sub": 1 - sub}).wait_recv()
                p_scr[...] = d_recv[...].astype(F32)
            behind = unfold(p_scr[...]).reshape(rows, cols, ch)
            before = [origin + (0.5 * size[0]) * behind] + [origin + a for a in after[:-1]]
            for r in range(rows):
                for n in range(steps):
                    start = r * block + n * cols
                    u_scr[start:start + cols, :] = before[n][r].astype(BF16).astype(F32)
            send_halo(sweep + 1)
            own_rows()

    for sweep in range(ITERS):
        for side, there in ((0, has_low), (1, has_high)):
            @pl.when(there)
            def _():
                halo_copy(sweep, side).wait_send()
        for k in range(1, n_tm):
            @pl.when(k > z)
            def _():
                t_copy(sweep, k).wait_send()
        s_copy(sweep).wait_send()
    @pl.when((sub == 0) | next_z)
    def _():
        d_copy({"sub": 1 - sub}).wait_send()


def shards(n_chan, n_tm, start_state, guess, w_in, w_mid, w_out, time_embed, levels, plan, offset):
    steps, rows, merged = guess.shape
    ch = w_out.shape[1]
    hid = w_in.shape[1]
    cols = merged // ch
    block = steps * cols
    two = n_chan == 2 and rows == 4
    cfg = (steps, rows, cols, ch, hid, n_chan, n_tm, levels.shape[0], plan.shape[0], two)
    n_in = rows + 4 if two else rows + 6
    n_x2 = n_in - 1 if two else n_in - 2
    n_x3 = n_in - 2 if two else n_in - 4
    vmem = pl.BlockSpec(memory_space=pltpu.VMEM)
    hbm = pl.BlockSpec(memory_space=pltpu.HBM)
    dma = pltpu.SemaphoreType.DMA
    half = rows * cols // 2
    out = pl.pallas_call(
        functools.partial(body, cfg),
        out_shape=jax.ShapeDtypeStruct(guess.shape, F32),
        in_specs=[hbm] * 9,
        out_specs=vmem,
        scratch_shapes=[
            pltpu.VMEM(start_state.shape, F32),
            pltpu.VMEM(guess.shape, BF16),
            pltpu.SMEM(levels.shape, F32),
            pltpu.SMEM(plan.shape, jnp.int32),
            pltpu.SMEM(offset.shape, jnp.int32),
            pltpu.VMEM(w_in.shape[::-1], BF16),
            pltpu.VMEM(w_mid.shape[::-1], BF16),
            pltpu.VMEM(w_out.shape[::-1], BF16),
            pltpu.VMEM(time_embed.shape[::-1], BF16),
            pltpu.VMEM((3, hid, 3 * ch), BF16),
            pltpu.VMEM((3, hid - hid % 128, 3 * hid), BF16),
            pltpu.VMEM((3 * (hid % 128), 3 * hid), BF16),
            pltpu.VMEM((3 * ch, 3 * hid), BF16),
            pltpu.VMEM((n_in * block, 3 * ch), BF16),
            pltpu.VMEM((n_x2 * block, 3 * hid), BF16),
            pltpu.VMEM((n_x3 * block, 3 * hid), BF16),
            pltpu.VMEM((rows * block, ch), F32),
            pltpu.VMEM((rows * cols, ch), F32),
            pltpu.VMEM((rows * block, ch), F32),
            pltpu.VMEM((half, 2 * ch), F32),
            pltpu.VMEM((ITERS, 2, 3 * block // 2, 2 * ch), BF16),
            pltpu.VMEM((ITERS, 2, 3 * block // 2, 2 * ch), BF16),
            pltpu.VMEM((ITERS, half, 2 * ch), BF16),
            pltpu.VMEM((ITERS, n_tm, half, 2 * ch), BF16),
            pltpu.VMEM((ITERS, half, 2 * ch), F32),
            pltpu.VMEM((ITERS, half, 2 * ch), F32),
            pltpu.VMEM((half, 2 * ch), BF16),
            pltpu.VMEM((half, 2 * ch), BF16),
            dma((9,)),
            dma((ITERS, 2)),
            dma((ITERS, 2)),
            dma((ITERS, n_tm)),
            dma((ITERS, n_tm)),
            dma((ITERS,)),
            dma((ITERS,)),
            dma,
            dma,
        ],
        compiler_params=pltpu.CompilerParams(
            collective_id=0, has_side_effects=True, vmem_limit_bytes=60 * 1024 * 1024
        ),
    )(start_state, guess, levels, plan, offset, w_in.T, w_mid.T, w_out.T, time_embed.T)
    return out


def solution(mesh):
    return jax.shard_map(
        functools.partial(shards, mesh.shape["chan"], mesh.shape["tm"]),
        mesh=mesh,
        in_specs=(
            P(("parts", "chan"), None),
            P(("parts", "tm", "sub"), "chan", None),
            P(),
            P(),
            P(),
            P(),
            P(),
            P("parts"),
            P("parts"),
        ),
        out_specs=P(("parts", "tm", "sub"), "chan", None),
        check_vma=False,
    )
```
